32 devices in a mesh: section: 8 (over y, x, core), kv: 4 (over z).
Axes of the slice: x: 2, y: 2, z: 4, core: 2. Of those that a mesh axis runs over, the one named last changes fastest.
Arguments:
- query: bfloat16 [8, 512, 4096], P('section', None, 'kv'), parts along dimension 2, may hold values from -6 to 6
- grad_output: bfloat16 [8, 512, 4096], P('section', None, 'kv'), parts along dimension 2, may hold values from -150 to 150
- log_total: bfloat16 [8, 512, 32], P('section', None, 'kv'), parts along dimension 2, may hold values from -1 to 10, as said below
- offset: bfloat16 [8, 512, 32], P('section', None, 'kv'), parts along dimension 2, may hold values from -600 to 600
- slice_keys: bfloat16 [8, 512, 1024], P('section', None, 'kv'), parts along dimension 2, may hold values from -7 to 7
- pool_keys: bfloat16 [8, 1536, 1024], P('section', None, 'kv'), parts along dimension 2, may hold values from -7 to 7
- block_table: int32 [8, 3], P('section'), may hold values from 0 to 2, each once within a row
Outputs:
- query_grad: bfloat16 [8, 512, 4096], P('section', None, 'kv'), parts along dimension 2
- slice_grad: bfloat16 [8, 512, 1024], P('section', None, 'kv'), parts along dimension 2
- pool_grad: bfloat16 [8, 1536, 1024], P('section', None, 'kv'), parts along dimension 2
The draws below stay inside these ranges and needn't reach their ends.
There are 4 independent parts, one for each index of `kv`. The reference program is written for one: setup_inputs(seed, part) draws one part's arguments, and reference() takes and returns one part's arrays. A program takes and returns all parts, laid end to end along the dimension named above; an argument that names none is the same for every part. Nothing has to cross between parts.
Inputs may be any that keep to these rules, and one draw needn't show every extreme that they name: Each row of block_table names every slot 0 to 2 once. log_total lies near the log of the count of visible keys of the row plus one half.
All inputs are finite; a program needn't handle non-finite values.
Results may differ from the reference program's by a relative error of at most 0.0051.
Values may be sent and summed in bfloat16 or wider, within the bound.
A program may use at most 128 MiB of HBM per device.

```python
import jax
import jax.numpy as jnp
from jax import lax

HQ = 8
DH = 128
BLK = 512
NSL = 4
POOL = 3
LAYERS = 8


def draw_log_total(key, part):
    second_key = jax.random.fold_in(jax.random.fold_in(key, 17), 1)
    layer_ids = jnp.arange(LAYERS, dtype=jnp.int32)[:, None, None]
    slice_depth = NSL - 1 - layer_ids // (LAYERS // NSL) % (NSL - 1)
    row_ids = jnp.arange(BLK, dtype=jnp.int32)[None, :, None]
    visible = (slice_depth * BLK + row_ids + 1).astype(jnp.float32)
    noise = jax.random.uniform(second_key, (LAYERS, BLK, HQ), jnp.float32, -1.0, 1.0)
    return (jnp.log(visible) + 0.5 + noise).astype(jnp.bfloat16)


def block_scale(key, dims, cuts, low, largest):
    factor_of = 1.0
    for dim, blocks in cuts:
        draws = jax.random.uniform(jax.random.fold_in(jax.random.fold_in(key, 6), dim), (blocks,), jnp.float32, low / len(cuts), largest / len(cuts))
        factor_of = factor_of * jnp.repeat(jnp.exp(draws), dims[dim] // blocks).reshape((-1,) + (1,) * (len(dims) - 1 - dim))
    return factor_of


def centred(key, dims, scale, bound, shards=(), kind=jnp.bfloat16):
    array = scale * jax.random.normal(key, dims, jnp.float32)
    if shards:
        array = array * block_scale(key, dims, shards, -0.22, 0.18)
    return jnp.clip(array, -bound, bound).astype(kind)


def setup_inputs(seed: int = 0, part: int = 0) -> dict:
    streams_of = jax.random.split(jax.random.key(seed), 8)
    own_keys = jax.random.split(jax.random.fold_in(streams_of[7], part), 8)
    return {
        "query": centred(own_keys[0], (LAYERS, BLK, HQ * DH), 1.0, 6.0, ((0, 8),)),
        "grad_output": centred(own_keys[1], (LAYERS, BLK, HQ * DH), 25.0, 150.0, ((0, 8),)),
        "log_total": draw_log_total(jax.random.fold_in(jax.random.fold_in(streams_of[7], part), 71), part),
        "offset": centred(own_keys[3], (LAYERS, BLK, HQ), 100.0, 600.0, ((0, 8),)),
        "slice_keys": centred(own_keys[4], (LAYERS, BLK, 2 * DH), 1.2, 7.0, ((0, 8),)),
        "pool_keys": centred(own_keys[5], (LAYERS, POOL * BLK, 2 * DH), 1.2, 7.0, ((0, 8),)),
        "block_table": jax.vmap(lambda own: jax.random.permutation(own, POOL))(jax.random.split(streams_of[6], LAYERS)).reshape((LAYERS, POOL)).astype(jnp.int32),
    }


def block_terms(queries, out_grads, totals, offsets, key_data, value_data, causal):
    score_scale = DH ** -0.5
    scores = jnp.einsum("rhd,cd->rhc", queries.astype(jnp.float32), key_data.astype(jnp.float32)) * score_scale
    weights = jnp.exp(scores - totals.astype(jnp.float32)[:, :, None])
    if causal:
        row_ids = jnp.arange(queries.shape[0], dtype=jnp.int32)
        visible = row_ids[:, None] >= row_ids[None, :]
        weights = jnp.where(visible[:, None, :], weights, jnp.zeros_like(weights))
    weight_grad = jnp.einsum("rhd,cd->rhc", out_grads.astype(jnp.float32), value_data.astype(jnp.float32))
    score_grad = weights * (weight_grad - offsets.astype(jnp.float32)[:, :, None])
    weights_low, score_low = lax.optimization_barrier((weights.astype(jnp.bfloat16), score_grad.astype(jnp.bfloat16)))
    query_part = jnp.einsum("rhc,cd->rhd", score_low.astype(jnp.float32), key_data.astype(jnp.float32)) * score_scale
    key_part = jnp.einsum("rhc,rhd->cd", score_low.astype(jnp.float32), queries.astype(jnp.float32)) * score_scale
    value_part = jnp.einsum("rhc,rhd->cd", weights_low.astype(jnp.float32), out_grads.astype(jnp.float32))
    return query_part, jnp.concatenate([key_part, value_part], axis=1)


def reference(query, grad_output, log_total, offset, slice_keys, pool_keys, block_table):
    group_size = LAYERS // NSL
    half_layers = LAYERS // 2

    def one_layer(layer_index):
        slice_depth = (NSL - 1) - (layer_index // group_size) % (NSL - 1)
        holder = (layer_index + half_layers) % LAYERS
        queries = query[layer_index].reshape(BLK, HQ, DH)
        out_grads = grad_output[layer_index].reshape(BLK, HQ, DH)
        totals = log_total[layer_index]
        offsets = offset[layer_index]
        own_block = slice_keys[layer_index]
        pool_block = pool_keys[holder]
        own_query, own_grad = block_terms(queries, out_grads, totals, offsets, own_block[:, :DH], own_block[:, DH:], True)
        pool_query = jnp.zeros((BLK, HQ, DH), jnp.float32)
        pool_sum = jnp.zeros((POOL * BLK, 2 * DH), jnp.float32)
        for position in range(POOL):
            pool_slot = block_table[holder, position]
            row_start = (pool_slot * BLK).astype(jnp.int32)
            key_block = lax.dynamic_slice_in_dim(pool_block, row_start, BLK, 0)
            query_part, block_grad = block_terms(queries, out_grads, totals, offsets, key_block[:, :DH], key_block[:, DH:], False)
            in_use = (position < slice_depth).astype(jnp.float32)
            pool_query = pool_query + in_use * query_part
            pool_sum = lax.dynamic_update_slice_in_dim(pool_sum, in_use * block_grad, row_start, 0)
        pool_term = lax.optimization_barrier(pool_query.astype(jnp.bfloat16)).astype(jnp.float32)
        query_sum = own_query + pool_term
        return (query_sum.reshape(BLK, HQ * DH).astype(jnp.bfloat16), own_grad.astype(jnp.bfloat16), pool_sum.astype(jnp.bfloat16))

    layers = jnp.arange(LAYERS, dtype=jnp.int32)
    query_grad, slice_grad, pool_sums = lax.map(one_layer, layers)
    pool_grad = jnp.roll(pool_sums, half_layers, axis=0)
    return query_grad, slice_grad, pool_grad
```

```python
import functools
import math

import jax
import jax.numpy as jnp
from jax import lax
from jax.experimental import pallas as pl
from jax.experimental.pallas import tpu as pltpu
from jax.sharding import PartitionSpec as P

PARTS = 1
LOG2E = math.log2(math.e)


def dot(a, b, ca, cb):
    return lax.dot_general(
        a, b, (((ca,), (cb,)), ((), ())), preferred_element_type=jnp.float32
    )


def kernel(
    slots, heads, table, q_hbm, g_hbm, lt_hbm, off_hbm, own_hbm, pool_hbm,
    dq_hbm, down_hbm, dpool_hbm,
    q, g, lt, off, own, pool, staged, arrived, outgoing, returned,
    dq, dq_low, dk, dv, down, dpool, lt_t, off_t,
    in_sem, out_sem, ksend, krecv, gsend, grecv,
):
    chunk = staged.shape[1]
    parts = staged.shape[0] // slots
    rows = q.shape[0]
    head = own.shape[1] // 2
    half = rows // 2
    scale = head ** (-0.5)
    sections = lax.axis_size("section")
    group = sections // (slots + 1)
    me = lax.axis_index("section")
    partner = lax.rem(me + sections // 2, sections)

    def chunks_of(layer):
        return parts * (slots - lax.rem(lax.div(layer, group), slots))

    mine, theirs = chunks_of(me), chunks_of(partner)

    ins = [
        pltpu.make_async_copy(src, dst, in_sem.at[n])
        for n, (src, dst) in enumerate(
            [(pool_hbm, pool), (own_hbm, own), (q_hbm, q), (g_hbm, g), (lt_hbm, lt), (off_hbm, off)]
        )
    ]
    for copy in ins:
        copy.start()
    barrier = pltpu.get_barrier_semaphore()
    pl.semaphore_signal(
        barrier, inc=1, device_id={"section": partner}, device_id_type=pl.DeviceIdType.MESH
    )
    ins[0].wait()
    for position in range(slots):
        for part in range(parts):
            staged[position * parts + part] = pool[table[0, position] * parts + part]
    pl.semaphore_wait(barrier, 1)

    def remote(src, dst, ssem, rsem, n):
        return pltpu.make_async_remote_copy(
            src_ref=src.at[n],
            dst_ref=dst.at[n],
            send_sem=ssem.at[n],
            recv_sem=rsem.at[n],
            device_id={"section": partner},
            device_id_type=pl.DeviceIdType.MESH,
        )

    def keys_copy(n):
        return remote(staged, arrived, ksend, krecv, n)

    def grads_copy(n):
        return remote(outgoing, returned, gsend, grecv, n)

    @pl.loop(0, theirs)
    def _(n):
        keys_copy(n).start()

    @pl.loop(theirs, slots * parts)
    def _(n):
        returned[n] = jnp.zeros(returned.shape[1:], returned.dtype)

    for copy in ins[1:]:
        copy.wait()
    lt_t[...] = lt[...].astype(jnp.float32) * LOG2E
    off_t[...] = off[...].astype(jnp.float32)

    def tile(key, value, h, first, mask):
        cols = slice(h * head, (h + 1) * head)
        qh = q[first:, cols]
        gh = g[first:, cols]
        scores = dot(key, qh, 1, 1)
        weights = jnp.exp2(scores * (scale * LOG2E) - lt_t[h : h + 1, first:])
        if mask is not None:
            weights = jnp.where(mask, weights, 0.0)
        grads = weights * (dot(value, gh, 1, 1) - off_t[h : h + 1, first:])
        weights_low = weights.astype(jnp.bfloat16)
        score_low = grads.astype(jnp.bfloat16)
        return (
            dot(score_low, key, 0, 0),
            dot(score_low, qh, 1, 0),
            dot(weights_low, gh, 1, 0),
        )

    for h in range(heads):
        cols = slice(h * head, (h + 1) * head)
        for t in range(2):
            first = t * half
            keys = slice(first, first + half)
            shape = (half, rows - first)
            mask = lax.broadcasted_iota(jnp.int32, shape, 1) >= lax.broadcasted_iota(
                jnp.int32, shape, 0
            )
            dq_t, dk_t, dv_t = tile(own[keys, :head], own[keys, head:], h, first, mask)
            if t == 0:
                dq[:, cols] = dq_t
            else:
                dq[first:, cols] += dq_t
            if h == 0:
                dk[keys] = dk_t
                dv[keys] = dv_t
            else:
                dk[keys] += dk_t
                dv[keys] += dv_t
    down[:, :head] = (dk[...] * scale).astype(down.dtype)
    down[:, head:] = dv[...].astype(down.dtype)
    down_out = pltpu.make_async_copy(down, down_hbm, out_sem.at[0])
    down_out.start()

    @pl.loop(0, mine)
    def _(n):
        keys_copy(n).wait_recv()
        for h in range(heads):
            cols = slice(h * head, (h + 1) * head)
            dq_t, dk_t, dv_t = tile(arrived[n, :, :head], arrived[n, :, head:], h, 0, None)
            dq[:, cols] += dq_t
            if h == 0:
                dk[:chunk] = dk_t
                dv[:chunk] = dv_t
            else:
                dk[:chunk] += dk_t
                dv[:chunk] += dv_t
        outgoing[n, :, :head] = (dk[:chunk] * scale).astype(outgoing.dtype)
        outgoing[n, :, head:] = dv[:chunk].astype(outgoing.dtype)
        grads_copy(n).start()

    dq_low[...] = (dq[...] * scale).astype(dq_low.dtype)
    dq_out = pltpu.make_async_copy(dq_low, dq_hbm, out_sem.at[1])
    dq_out.start()

    @pl.loop(0, theirs)
    def _(n):
        keys_copy(n).wait_send()
        grads_copy(n).wait_recv()

    for slot in range(slots):
        place = jnp.int32(0)
        for position in range(1, slots):
            place = jnp.where(table[0, position] == slot, position, place)
        for part in range(parts):
            dpool[slot * parts + part] = returned[place * parts + part]
    dpool_out = pltpu.make_async_copy(dpool, dpool_hbm, out_sem.at[2])
    dpool_out.start()

    @pl.loop(0, mine)
    def _(n):
        grads_copy(n).wait_send()

    down_out.wait()
    dq_out.wait()
    dpool_out.wait()


def per_device(query, grad_output, log_total, offset, slice_keys, pool_keys, block_table):
    rows, width = slice_keys.shape[1:]
    heads = log_total.shape[2]
    slots = block_table.shape[1]
    total = slots * PARTS
    chunk = rows // PARTS
    pool = pool_keys.reshape(total, chunk, width)
    low = jnp.bfloat16
    hbm = pl.BlockSpec(memory_space=pl.ANY)
    block = (total, chunk, width)
    dq, down, dpool = pl.pallas_call(
        functools.partial(kernel, slots, heads),
        out_shape=(
            jax.ShapeDtypeStruct(query.shape[1:], low),
            jax.ShapeDtypeStruct(slice_keys.shape[1:], low),
            jax.ShapeDtypeStruct(block, low),
        ),
        in_specs=[pl.BlockSpec(memory_space=pltpu.SMEM)] + [hbm] * 6,
        out_specs=(hbm, hbm, hbm),
        scratch_shapes=[
            pltpu.VMEM(query.shape[1:], low),
            pltpu.VMEM(query.shape[1:], low),
            pltpu.VMEM((heads, rows), low),
            pltpu.VMEM((heads, rows), low),
            pltpu.VMEM((rows, width), low),
            pltpu.VMEM(block, low),
            pltpu.VMEM(block, low),
            pltpu.VMEM(block, low),
            pltpu.VMEM(block, low),
            pltpu.VMEM(block, low),
            pltpu.VMEM(query.shape[1:], jnp.float32),
            pltpu.VMEM(query.shape[1:], low),
            pltpu.VMEM((rows, width // 2), jnp.float32),
            pltpu.VMEM((rows, width // 2), jnp.float32),
            pltpu.VMEM((rows, width), low),
            pltpu.VMEM(block, low),
            pltpu.VMEM((heads, rows), jnp.float32),
            pltpu.VMEM((heads, rows), jnp.float32),
            pltpu.SemaphoreType.DMA((6,)),
            pltpu.SemaphoreType.DMA((3,)),
            pltpu.SemaphoreType.DMA((total,)),
            pltpu.SemaphoreType.DMA((total,)),
            pltpu.SemaphoreType.DMA((total,)),
            pltpu.SemaphoreType.DMA((total,)),
        ],
        compiler_params=pltpu.CompilerParams(
            collective_id=0, has_side_effects=True, vmem_limit_bytes=48 * 1024 * 1024
        ),
        name="grads",
    )(block_table, query[0], grad_output[0], log_total[0].T, offset[0].T, slice_keys[0], pool)
    return dq[None], down[None], dpool.reshape(pool_keys.shape)


def solution(mesh):
    lanes = P("section", None, "kv")
    return jax.shard_map(
        per_device,
        mesh=mesh,
        in_specs=(lanes,) * 6 + (P("section", None),),
        out_specs=(lanes,) * 3,
        check_vma=False,
    )
```

```python
import functools
import math

import jax
import jax.numpy as jnp
from jax import lax
from jax.experimental import pallas as pl
from jax.experimental.pallas import tpu as pltpu
from jax.sharding import PartitionSpec as P

PARTS = 1
LOG2E = math.log2(math.e)


def dot(a, b, ca, cb):
    return lax.dot_general(
        a, b, (((ca,), (cb,)), ((), ())), preferred_element_type=jnp.float32
    )


def kernel(
    slots, heads, table, q_hbm, g_hbm, lt_hbm, off_hbm, own_hbm, pool_hbm,
    dq_hbm, down_hbm, returned,
    q, g, lt, off, own, pool, staged, arrived, outgoing,
    dq, dk, dv, dq_low, down, zeros, lt_t, off_t,
    in_sem, out_sem, zero_sem, ksend, krecv, gsend, grecv,
):
    chunk = staged.shape[1]
    parts = staged.shape[0] // slots
    rows = q.shape[0]
    head = own.shape[1] // 2
    half = rows // 2
    scale = head ** (-0.5)
    sections = lax.axis_size("section")
    group = sections // (slots + 1)
    me = lax.axis_index("section")
    partner = lax.rem(me + sections // 2, sections)

    def chunks_of(layer):
        return parts * (slots - lax.rem(lax.div(layer, group), slots))

    mine, theirs = chunks_of(me), chunks_of(partner)

    ins = [
        pltpu.make_async_copy(src, dst, in_sem.at[n])
        for n, (src, dst) in enumerate(
            [(pool_hbm, pool), (own_hbm, own), (q_hbm, q), (g_hbm, g), (lt_hbm, lt), (off_hbm, off)]
        )
    ]
    for copy in ins:
        copy.start()
    barrier = pltpu.get_barrier_semaphore()
    pl.semaphore_signal(
        barrier, inc=1, device_id={"section": partner}, device_id_type=pl.DeviceIdType.MESH
    )
    ins[0].wait()
    for position in range(slots):
        for part in range(parts):
            staged[position * parts + part] = pool[table[0, position] * parts + part]
    pl.semaphore_wait(barrier, 1)

    def remote(src, dst, ssem, rsem, n):
        return pltpu.make_async_remote_copy(
            src_ref=src.at[n],
            dst_ref=dst.at[n],
            send_sem=ssem.at[n],
            recv_sem=rsem.at[n],
            device_id={"section": partner},
            device_id_type=pl.DeviceIdType.MESH,
        )

    def keys_copy(n):
        return remote(staged, arrived, ksend, krecv, n)

    def grads_copy(n):
        return remote(outgoing, returned, gsend, grecv, n)

    def zero_copy(n):
        return pltpu.make_async_copy(zeros, returned.at[n], zero_sem.at[n])

    @pl.loop(0, theirs)
    def _(n):
        keys_copy(n).start()

    zeros[...] = jnp.zeros(zeros.shape, zeros.dtype)

    @pl.loop(theirs, slots * parts)
    def _(n):
        zero_copy(n).start()

    for copy in ins[1:]:
        copy.wait()
    lt_t[...] = lt[...].astype(jnp.float32) * LOG2E
    off_t[...] = off[...].astype(jnp.float32)

    def tile(key, value, h, first, mask):
        cols = slice(h * head, (h + 1) * head)
        qh = q[first:, cols]
        gh = g[first:, cols]
        scores = dot(key, qh, 1, 1)
        weights = jnp.exp2(scores * (scale * LOG2E) - lt_t[h : h + 1, first:])
        if mask is not None:
            weights = jnp.where(mask, weights, 0.0)
        grads = weights * (dot(value, gh, 1, 1) - off_t[h : h + 1, first:])
        weights_low = weights.astype(jnp.bfloat16)
        score_low = grads.astype(jnp.bfloat16)
        return (
            dot(key, score_low, 0, 0),
            dot(score_low, qh, 1, 0),
            dot(weights_low, gh, 1, 0),
        )

    for h in range(heads):
        cols = slice(h * head, (h + 1) * head)
        for t in range(2):
            first = t * half
            keys = slice(first, first + half)
            shape = (half, rows - first)
            mask = lax.broadcasted_iota(jnp.int32, shape, 1) >= lax.broadcasted_iota(
                jnp.int32, shape, 0
            )
            dq_t, dk_t, dv_t = tile(own[keys, :head], own[keys, head:], h, first, mask)
            if t == 0:
                dq[cols] = dq_t
            else:
                dq[cols, first:] += dq_t
            if h == 0:
                dk[keys] = dk_t
                dv[keys] = dv_t
            else:
                dk[keys] += dk_t
                dv[keys] += dv_t
    down[:, :head] = (dk[...] * scale).astype(down.dtype)
    down[:, head:] = dv[...].astype(down.dtype)
    down_out = pltpu.make_async_copy(down, down_hbm, out_sem.at[0])
    down_out.start()

    @pl.loop(0, mine)
    def _(n):
        keys_copy(n).wait_recv()
        for h in range(heads):
            cols = slice(h * head, (h + 1) * head)
            dq_t, dk_t, dv_t = tile(arrived[n, :, :head], arrived[n, :, head:], h, 0, None)
            dq[cols] += dq_t
            if h == 0:
                dk[:chunk] = dk_t
                dv[:chunk] = dv_t
            else:
                dk[:chunk] += dk_t
                dv[:chunk] += dv_t
        outgoing[n, :, :head] = (dk[:chunk] * scale).astype(outgoing.dtype)
        outgoing[n, :, head:] = dv[:chunk].astype(outgoing.dtype)
        grads_copy(n).start()

    for h in range(heads):
        cols = slice(h * head, (h + 1) * head)
        dq_low[:, cols] = (dq[cols].T * scale).astype(dq_low.dtype)
    dq_out = pltpu.make_async_copy(dq_low, dq_hbm, out_sem.at[1])
    dq_out.start()

    @pl.loop(0, theirs)
    def _(n):
        keys_copy(n).wait_send()
        grads_copy(n).wait_recv()

    @pl.loop(0, mine)
    def _(n):
        grads_copy(n).wait_send()

    @pl.loop(theirs, slots * parts)
    def _(n):
        zero_copy(n).wait()

    down_out.wait()
    dq_out.wait()


def finish(
    slots, table, dq, down, returned, dq_hbm, down_hbm, dpool_hbm, dq_low, down_low, pool, isem, osem
):
    parts = returned.shape[0] // slots
    ins, outs = [(dq, dq_low), (down, down_low)], [(dq_low, dq_hbm), (down_low, down_hbm)]
    for slot in range(slots):
        place = jnp.int32(0)
        for position in range(1, slots):
            place = jnp.where(table[0, position] == slot, position, place)
        block = pl.ds(slot * parts, parts)
        ins.append((returned.at[pl.ds(place * parts, parts)], pool.at[block]))
        outs.append((pool.at[block], dpool_hbm.at[block]))
    ins = [
        pltpu.make_async_copy(src, dst, isem.at[n]) for n, (src, dst) in enumerate(ins)
    ]
    outs = [
        pltpu.make_async_copy(src, dst, osem.at[n]) for n, (src, dst) in enumerate(outs)
    ]
    for copy in ins:
        copy.start()
    for first, second in zip(ins, outs):
        first.wait()
        second.start()
    for copy in outs:
        copy.wait()


def per_device(query, grad_output, log_total, offset, slice_keys, pool_keys, block_table):
    rows, width = slice_keys.shape[1:]
    heads = log_total.shape[2]
    slots = block_table.shape[1]
    total = slots * PARTS
    chunk = rows // PARTS
    pool = pool_keys.reshape(total, chunk, width)
    low = jnp.bfloat16
    smem = pl.BlockSpec(memory_space=pltpu.SMEM)
    anywhere = pl.BlockSpec(memory_space=pl.ANY)
    block = (total, chunk, width)
    results = (
        jax.ShapeDtypeStruct(query.shape[1:], low),
        jax.ShapeDtypeStruct(slice_keys.shape[1:], low),
        jax.ShapeDtypeStruct(block, low),
    )
    held = pl.pallas_call(
        functools.partial(kernel, slots, heads),
        out_shape=results,
        in_specs=[smem] + [anywhere] * 6,
        out_specs=(anywhere,) * 3,
        scratch_shapes=[
            pltpu.VMEM(query.shape[1:], low),
            pltpu.VMEM(query.shape[1:], low),
            pltpu.VMEM((heads, rows), low),
            pltpu.VMEM((heads, rows), low),
            pltpu.VMEM((rows, width), low),
            pltpu.VMEM(block, low),
            pltpu.VMEM(block, low),
            pltpu.VMEM(block, low),
            pltpu.VMEM(block, low),
            pltpu.VMEM((query.shape[2], rows), jnp.float32),
            pltpu.VMEM((rows, width // 2), jnp.float32),
            pltpu.VMEM((rows, width // 2), jnp.float32),
            pltpu.VMEM(query.shape[1:], low),
            pltpu.VMEM((rows, width), low),
            pltpu.VMEM((chunk, width), low),
            pltpu.VMEM((heads, rows), jnp.float32),
            pltpu.VMEM((heads, rows), jnp.float32),
            pltpu.SemaphoreType.DMA((6,)),
            pltpu.SemaphoreType.DMA((2,)),
            pltpu.SemaphoreType.DMA((total,)),
            pltpu.SemaphoreType.DMA((total,)),
            pltpu.SemaphoreType.DMA((total,)),
            pltpu.SemaphoreType.DMA((total,)),
            pltpu.SemaphoreType.DMA((total,)),
        ],
        compiler_params=pltpu.CompilerParams(
            collective_id=0, has_side_effects=True, vmem_limit_bytes=56 * 1024 * 1024
        ),
        name="grads",
    )(block_table, query[0], grad_output[0], log_total[0].T, offset[0].T, slice_keys[0], pool)
    dq, down, dpool = pl.pallas_call(
        functools.partial(finish, slots),
        out_shape=results,
        in_specs=[smem] + [anywhere] * 3,
        out_specs=(anywhere,) * 3,
        scratch_shapes=[
            pltpu.VMEM(query.shape[1:], low),
            pltpu.VMEM((rows, width), low),
            pltpu.VMEM(block, low),
            pltpu.SemaphoreType.DMA((2 + slots,)),
            pltpu.SemaphoreType.DMA((2 + slots,)),
        ],
        compiler_params=pltpu.CompilerParams(vmem_limit_bytes=56 * 1024 * 1024),
        name="finish",
    )(block_table, *held)
    return dq[None], down[None], dpool.reshape(pool_keys.shape)


def solution(mesh):
    lanes = P("section", None, "kv")
    return jax.shard_map(
        per_device,
        mesh=mesh,
        in_specs=(lanes,) * 6 + (P("section", None),),
        out_specs=(lanes,) * 3,
        check_vma=False,
    )
```
